512 devices in a mesh: src: 32 (over y_lo, z), tp: 16 (over x, y_hi, core).
Axes of the slice: x: 4, y: 4 (y_hi: 2, y_lo: 2; y = y_hi * 2 + y_lo), z: 16, core: 2. Of those that a mesh axis runs over, the one named last changes fastest.
Arguments:
- stream: float32 [64, 16384], P(None, 'src'), may hold values from -32 to 32
- norm_gain: float32 [16384], P('src'), may hold values from 0.1 to 1.9
- frozen_up_weight: bfloat16 [16384, 28672], P('src', 'tp'), may hold values from -0.046875 to 0.046875
- factor_a: bfloat16 [64, 16384], P('tp', 'src'), may hold values from -0.046875 to 0.046875
- factor_b: bfloat16 [64, 28672], P('src', 'tp'), may hold values from -0.1796875 to 0.1796875
- down_projection_matrix: bfloat16 [28672, 16384], P('tp', 'src'), may hold values from -0.03125 to 0.03125
Outputs:
- final_stream: float32 [64, 16384], P(None, 'src')
The draws below stay inside these ranges and needn't reach their ends.
All inputs are finite; a program needn't handle non-finite values.
Results may differ from the reference program's by a relative error of at most 0.0037.
Values may be sent and summed in bfloat16 or wider, within the bound.
No kernel may reach another device: no remote copies, remote signals or barrier semaphores. Data moves between devices by JAX's collectives and lax.ppermute only.
A program may use at most 64 MiB of HBM per device.

```python
import math
import jax
import jax.numpy as jnp
from jax import lax

D = 16384
FF = 28672
R = 64
ROWS = 64
STEPS = 3


def draw_stream(key, part):
    key = jax.random.fold_in(key, 1)
    key_base, key_cols, key_rows = jax.random.split(key, 3)
    ramp = 3.0 ** (jnp.arange(D, dtype=jnp.float32) / D)
    columns = ramp * jnp.exp(jax.random.uniform(key_cols, (D,), jnp.float32, 0.0, math.log(3.3)))
    base = jnp.clip(jax.random.normal(key_base, (ROWS, D), jnp.float32), -4.0, 4.0)
    rows = 0.075 * jnp.exp(jax.random.uniform(key_rows, (ROWS, 1), jnp.float32, 0.0, math.log(10.0)))
    return (base * rows * columns).astype(jnp.float32)


def level_of(rng, dims, cuts, least, high):
    loudness, own = 1.0, jax.random.fold_in(rng, 6)
    for dim, parts in cuts:
        draws = jnp.exp(jax.random.uniform(jax.random.fold_in(own, dim), (parts,), jnp.float32, least / len(cuts), high / len(cuts)))
        loudness = loudness * jnp.repeat(draws, dims[dim] // parts).reshape([-1 if axis == dim else 1 for axis in range(len(dims))])
    return loudness


def gaussian(stream_key, extent, spread, most, cuts=(), held_as=jnp.bfloat16):
    level = level_of(stream_key, extent, cuts, -0.22, 0.18) if cuts else 1.0
    drawn = jax.random.normal(stream_key, extent, jnp.float32) * spread * level
    return jnp.minimum(jnp.maximum(drawn, -most), most).astype(held_as)


def setup_inputs(seed: int = 0) -> dict:
    key_of = jax.random.split(jax.random.key(seed), 7)
    stream = draw_stream(jax.random.fold_in(key_of[6], 71), 0)
    norm_gain = jnp.clip(1.0 + 0.18 * jax.random.normal(key_of[1], (D,), jnp.float32), 0.1, 1.9)
    frozen_up_weight = gaussian(key_of[2], (D, FF), D ** -0.5, 0.046875, ((0, 32), (1, 16)))
    factor_a = gaussian(key_of[3], (R, D), D ** -0.5, 0.046875, ((0, 16), (1, 32)))
    factor_b = gaussian(key_of[4], (R, FF), 0.03, 0.1796875, ((0, 32), (1, 16)))
    down_projection_matrix = gaussian(key_of[5], (FF, D), FF ** -0.5, 0.03125, ((0, 16), (1, 32)))
    return dict(stream=stream, norm_gain=norm_gain, frozen_up_weight=frozen_up_weight, factor_a=factor_a, factor_b=factor_b, down_projection_matrix=down_projection_matrix)


ADAPTER_SCALING = 2.0
EPSILON = 1e-05

def reference(stream, norm_gain, frozen_up_weight, factor_a, factor_b, down_projection_matrix):
    blocks = 16
    base_blocks = frozen_up_weight.reshape(blocks, D // blocks, FF)
    rows_a = jnp.transpose(factor_a).reshape(blocks, D // blocks, R)

    def merge_block(factor_couple):
        low_rank_update = jnp.dot(factor_couple[1], factor_b, preferred_element_type=jnp.float32)
        return (factor_couple[0].astype(jnp.float32) + ADAPTER_SCALING * low_rank_update).astype(jnp.bfloat16)
    merged_up_weight = lax.map(merge_block, (base_blocks, rows_a)).reshape(D, FF)
    current = stream
    for step in range(STEPS):
        squares = lax.optimization_barrier(jnp.mean(current * current, axis=1, keepdims=True))
        scaled = (current * norm_gain).astype(jnp.bfloat16)
        hidden = jnp.dot(scaled, merged_up_weight, preferred_element_type=jnp.float32) * lax.rsqrt(squares + EPSILON)
        active = jax.nn.silu(hidden).astype(jnp.bfloat16)
        current = current + jnp.dot(active, down_projection_matrix, preferred_element_type=jnp.float32)
    return current
```

```python
import jax
import jax.numpy as jnp
from jax import lax
from jax.sharding import PartitionSpec as P

D = 16384
STEPS = 3
LANES = 128

ADAPTER_SCALING = 2.0
EPSILON = 1e-05

NEAR = [[y * 16 + far * 4 + low for y in range(2) for low in range(4)] for far in range(4)]
FAR = [[y * 16 + far * 4 + low for far in range(4)] for y in range(2) for low in range(4)]
CORES = [[2 * chip, 2 * chip + 1] for chip in range(8)]
CHIPS = [[2 * chip + core for chip in range(8)] for core in range(2)]


def exchange(blocks, axis, groups):
    return lax.all_to_all(blocks, axis, 0, 0, axis_index_groups=groups, tiled=True)


def share(block, axis, groups, size):
    return exchange(jnp.broadcast_to(block[None], (size,) + block.shape), axis, groups)


def total(blocks):
    return jnp.sum(blocks.astype(jnp.float32), axis=0)


def with_squares(values, squares):
    high = lax.reduce_precision(squares, 8, 7)
    rest = squares - high
    middle = lax.reduce_precision(rest, 8, 7)
    low = rest - middle
    parts = jnp.concatenate(
        [high, middle, low, jnp.zeros((values.shape[0], LANES - 3), jnp.float32)], axis=1
    )
    return jnp.concatenate([values, parts], axis=1).astype(jnp.bfloat16)


def split_squares(both):
    values, parts = both[:, :-LANES], both[:, -LANES:]
    return values, jnp.sum(parts[:, :3], axis=1, keepdims=True)


def per_device(stream, norm_gain, frozen_up_weight, factor_a, factor_b, down_projection_matrix):
    rows, width = stream.shape
    hidden_units = frozen_up_weight.shape[1]
    ranks_a = share(factor_a, "tp", None, 16).reshape(-1, width)
    ranks_b = share(factor_b, "src", None, 32).reshape(-1, hidden_units)
    low_rank_update = lax.dot_general(
        ranks_a, ranks_b, (((0,), (0,)), ((), ())), preferred_element_type=jnp.float32
    )
    merged_up_weight = (
        frozen_up_weight.astype(jnp.float32) + ADAPTER_SCALING * low_rank_update
    ).astype(jnp.bfloat16)
    current = stream
    for step in range(STEPS):
        local_squares = jnp.sum(current * current, axis=1, keepdims=True)
        scaled = (current * norm_gain).astype(jnp.bfloat16)
        partial_up = jnp.dot(scaled, merged_up_weight, preferred_element_type=jnp.float32)
        sent = with_squares(partial_up, local_squares)
        near = total(exchange(sent.reshape(8, rows // 8, -1), "src", NEAR))
        near_values, near_squares = split_squares(near)
        far = total(share(with_squares(near_values, near_squares), "src", FAR, 4))
        combined_output, squares = split_squares(far)
        hidden = combined_output * lax.rsqrt(squares / D + EPSILON)
        active = jax.nn.silu(hidden).astype(jnp.bfloat16)
        active = share(active, "src", NEAR, 8).reshape(rows, hidden_units)
        branch = jnp.dot(active, down_projection_matrix, preferred_element_type=jnp.float32)
        branch = total(share(branch.astype(jnp.bfloat16), "tp", CORES, 2))
        branch = total(share(branch.astype(jnp.bfloat16), "tp", CHIPS, 8))
        current = current + branch
    return current


def solution(mesh):
    in_specs = (
        P(None, "src"),
        P("src"),
        P("src", "tp"),
        P("tp", "src"),
        P("src", "tp"),
        P("tp", "src"),
    )
    out_specs = P(None, "src")
    return jax.shard_map(
        per_device, mesh=mesh, in_specs=in_specs, out_specs=out_specs, check_vma=False
    )
```

```python
import jax
import jax.numpy as jnp
from jax import lax
from jax.sharding import PartitionSpec as P

D = 16384
STEPS = 3
LANES = 128

ADAPTER_SCALING = 2.0
EPSILON = 1e-05

NEAR = [[y * 16 + far * 4 + low for y in range(2) for low in range(4)] for far in range(4)]
FAR = [[y * 16 + far * 4 + low for far in range(4)] for y in range(2) for low in range(4)]
PAIRS = [
    [src * 16 + chip * 2 + core for core in range(2) for src in near]
    for near in NEAR
    for chip in range(8)
]
CORES = [[2 * chip, 2 * chip + 1] for chip in range(8)]
CHIPS = [[2 * chip + core for chip in range(8)] for core in range(2)]
SWAP = [(i, i ^ 1) for i in range(16)]


def exchange(blocks, axis, groups):
    return lax.all_to_all(blocks, axis, 0, 0, axis_index_groups=groups, tiled=True)


def share(block, axis, groups, size):
    return exchange(jnp.broadcast_to(block[None], (size,) + block.shape), axis, groups)


def total(blocks):
    return jnp.sum(blocks.astype(jnp.float32), axis=0)


def pack(values, squares, others=None):
    high = lax.reduce_precision(squares, 8, 7)
    rest = squares - high
    middle = lax.reduce_precision(rest, 8, 7)
    parts = [values, high, middle, rest - middle]
    used = 3
    if others is not None:
        parts.append(others)
        used += others.shape[1]
    parts.append(jnp.zeros((values.shape[0], LANES - used), jnp.float32))
    return jnp.concatenate(parts, axis=1).astype(jnp.bfloat16)


def unpack(both, width):
    return both[:, :width], jnp.sum(both[:, width : width + 3], axis=1, keepdims=True)


def activate(values, squares):
    hidden = values * lax.rsqrt(squares / D + EPSILON)
    return jax.nn.silu(hidden).astype(jnp.bfloat16)


def dot(a, b):
    return jnp.dot(a, b, preferred_element_type=jnp.float32)


def per_device(stream, norm_gain, frozen_up_weight, factor_a, factor_b, down_projection_matrix):
    rows, width = stream.shape
    units = frozen_up_weight.shape[1]
    half = rows // 2
    core = lax.axis_index("tp") % 2
    first = core == 0

    down_own = down_projection_matrix
    down_other = lax.ppermute(down_own, "tp", SWAP)

    ranks_a = share(factor_a, "tp", None, 16)
    ranks_a = ranks_a.reshape(2, 4, 4, 2, width).transpose(1, 0, 2, 3, 4).reshape(-1, width)
    ranks = ranks_a.shape[0]

    ordered = stream.reshape(2, 8, rows // 16, width).transpose(1, 0, 2, 3).reshape(rows, width)
    scaled = (ordered * norm_gain).astype(jnp.bfloat16)
    squares = jnp.sum(ordered * ordered, axis=1, keepdims=True)
    projected = lax.dot_general(
        scaled, ranks_a, (((1,), (1,)), ((), ())), preferred_element_type=jnp.float32
    )
    sent = pack(dot(scaled, frozen_up_weight), squares, projected).reshape(8, rows // 8, -1)
    own_b = jnp.pad(factor_b, ((0, 0), (0, LANES)))
    sent = jnp.concatenate([sent, jnp.broadcast_to(own_b[None], (8,) + own_b.shape)], axis=1)
    near = exchange(sent, "src", NEAR)
    near_sum = total(near[:, : rows // 8])
    near_b = near[:, rows // 8 :].reshape(-1, units + LANES)
    values, squares = unpack(near_sum, units)
    projected = near_sum[:, units + 3 : units + 3 + ranks]
    sent = jnp.concatenate([pack(values, squares, projected), near_b], axis=0)
    far = share(sent, "src", FAR, 4)
    far_sum = total(far[:, : rows // 8])
    ranks_b = far[:, rows // 8 :, :units].reshape(ranks, units)
    values, squares = unpack(far_sum, units)
    projected = far_sum[:, units + 3 : units + 3 + ranks]
    high = lax.reduce_precision(projected, 8, 7)
    both = jnp.concatenate([high, projected - high], axis=0).astype(jnp.bfloat16)
    update = dot(both, ranks_b)
    update = update[: rows // 8] + update[rows // 8 :]
    active = activate(values + ADAPTER_SCALING * update, squares)

    low_rank_update = lax.dot_general(
        ranks_a, ranks_b, (((0,), (0,)), ((), ())), preferred_element_type=jnp.float32
    )
    up_own = (
        frozen_up_weight.astype(jnp.float32) + ADAPTER_SCALING * low_rank_update
    ).astype(jnp.bfloat16)
    up_other = lax.ppermute(up_own, "tp", SWAP)

    sent = jnp.broadcast_to(
        active.reshape(2, 1, rows // 16, units), (2, 8, rows // 16, units)
    ).reshape(16, rows // 16, units)
    active = exchange(sent, ("src", "tp"), PAIRS).reshape(2, half, units)
    active_own = jnp.where(first, active[0], active[1])
    active_other = jnp.where(first, active[1], active[0])
    current = jnp.where(first, stream[:half], stream[half:])

    for step in range(STEPS):
        if step > 0:
            squares = jnp.sum(current * current, axis=1, keepdims=True)
            scaled = (current * norm_gain).astype(jnp.bfloat16)
            values = jnp.concatenate([dot(scaled, up_own), dot(scaled, up_other)], axis=1)
            sent = pack(values, squares).reshape(8, half // 8, -1)
            near = total(exchange(sent, "src", NEAR))
            far = total(share(pack(*unpack(near, 2 * units)), "src", FAR, 4))
            active = activate(*unpack(far, 2 * units))
            active = share(active, "src", NEAR, 8).reshape(half, 2 * units)
            active_own, active_other = active[:, :units], active[:, units:]
        branch = dot(active_own, down_own) + dot(active_other, down_other)
        current = current + total(share(branch.astype(jnp.bfloat16), "tp", CHIPS, 8))
    return share(current, "tp", CORES, 2).reshape(rows, width)


def solution(mesh):
    in_specs = (
        P(None, "src"),
        P("src"),
        P("src", "tp"),
        P("tp", "src"),
        P("src", "tp"),
        P("tp", "src"),
    )
    out_specs = P(None, "src")
    return jax.shard_map(
        per_device, mesh=mesh, in_specs=in_specs, out_specs=out_specs, check_vma=False
    )
```

```python
import jax
import jax.numpy as jnp
from jax import lax
from jax.experimental import pallas as pl
from jax.experimental.pallas import tpu as pltpu
from jax.sharding import PartitionSpec as P

D = 16384
STEPS = 3
LANES = 128

ADAPTER_SCALING = 2.0
EPSILON = 1e-05

NEAR = [[y * 16 + far * 4 + low for y in range(2) for low in range(4)] for far in range(4)]
FAR = [[y * 16 + far * 4 + low for far in range(4)] for y in range(2) for low in range(4)]
PAIRS = [
    [src * 16 + chip * 2 + core for core in range(2) for src in near]
    for near in NEAR
    for chip in range(8)
]
CORES = [[2 * chip, 2 * chip + 1] for chip in range(8)]
CHIPS = [[2 * chip + core for chip in range(8)] for core in range(2)]
SWAP = [(i, i ^ 1) for i in range(16)]


def exchange(blocks, axis, groups):
    return lax.all_to_all(blocks, axis, 0, 0, axis_index_groups=groups, tiled=True)


def share(block, axis, groups, size):
    return exchange(jnp.broadcast_to(block[None], (size,) + block.shape), axis, groups)


def total(blocks):
    return jnp.sum(blocks.astype(jnp.float32), axis=0)


def pack(values, squares, others=None):
    high = lax.reduce_precision(squares, 8, 7)
    rest = squares - high
    middle = lax.reduce_precision(rest, 8, 7)
    parts = [values, high, middle, rest - middle]
    used = 3
    if others is not None:
        parts.append(others)
        used += others.shape[1]
    parts.append(jnp.zeros((values.shape[0], LANES - used), jnp.float32))
    return jnp.concatenate(parts, axis=1).astype(jnp.bfloat16)


def unpack(both, width):
    return both[:, :width], jnp.sum(both[:, width : width + 3], axis=1, keepdims=True)


def activate(values, squares):
    hidden = values * lax.rsqrt(squares / D + EPSILON)
    return jax.nn.silu(hidden).astype(jnp.bfloat16)


def dot(a, b):
    return jnp.dot(a, b, preferred_element_type=jnp.float32)


def params():
    return pltpu.CompilerParams(vmem_limit_bytes=24 * 1024 * 1024)


VMEM = pl.BlockSpec(memory_space=pltpu.VMEM)
ANYWHERE = pl.BlockSpec(memory_space=pl.ANY)


def merge_kernel(up_ref, a_ref, b_ref, out_ref):
    update = dot(a_ref[...], b_ref[...])
    out_ref[...] = (
        up_ref[...].astype(jnp.float32) + ADAPTER_SCALING * update
    ).astype(jnp.bfloat16)


def merge(up, ranks_a, ranks_b):
    width, units = up.shape
    ranks = ranks_b.shape[0]
    block = units // 2
    return pl.pallas_call(
        merge_kernel,
        grid=(units // block,),
        in_specs=[
            pl.BlockSpec((width, block), lambda i: (0, i)),
            pl.BlockSpec((width, ranks), lambda i: (0, 0)),
            pl.BlockSpec((ranks, block), lambda i: (0, i)),
        ],
        out_specs=pl.BlockSpec((width, block), lambda i: (0, i)),
        out_shape=jax.ShapeDtypeStruct(up.shape, jnp.bfloat16),
        compiler_params=params(),
        cost_estimate=pl.CostEstimate(
            flops=2 * width * units * ranks, bytes_accessed=4 * width * units, transcendentals=0
        ),
    )(up, ranks_a.T, ranks_b)


def up_kernel(branch_ref, current_ref, gain_ref, own_ref, other_ref, next_ref, sent_ref, held, sems):
    units = own_ref.shape[1]
    part = units // 2
    copies = []
    for i in range(4):
        source = (own_ref, other_ref)[i // 2].at[:, pl.ds((i % 2) * part, part)]
        copies.append(pltpu.make_async_copy(source, held.at[i], sems.at[i]))
        copies[-1].start()
    current = current_ref[...] + jnp.sum(branch_ref[...].astype(jnp.float32), axis=0)
    next_ref[...] = current
    scaled = (current * gain_ref[...]).astype(jnp.bfloat16)
    squares = jnp.sum(current * current, axis=1, keepdims=True)
    high = squares.astype(jnp.bfloat16).astype(jnp.float32)
    rest = squares - high
    middle = rest.astype(jnp.bfloat16).astype(jnp.float32)
    lane = lax.broadcasted_iota(jnp.int32, (current.shape[0], LANES), 1)
    tail = jnp.where(lane == 0, high, jnp.where(lane == 1, middle, rest - middle))
    sent_ref[:, pl.ds(2 * units, LANES)] = jnp.where(lane < 3, tail, 0.0).astype(jnp.bfloat16)
    for i in range(4):
        copies[i].wait()
        sent_ref[:, pl.ds(i * part, part)] = dot(scaled, held[i]).astype(jnp.bfloat16)


def up(branches, current, gain, own, other):
    rows, width = current.shape
    units = own.shape[1]
    return pl.pallas_call(
        up_kernel,
        in_specs=[VMEM, VMEM, VMEM, ANYWHERE, ANYWHERE],
        out_specs=[VMEM, VMEM],
        out_shape=[
            jax.ShapeDtypeStruct(current.shape, jnp.float32),
            jax.ShapeDtypeStruct((rows, 2 * units + LANES), jnp.bfloat16),
        ],
        scratch_shapes=[
            pltpu.VMEM((4, width, units // 2), jnp.bfloat16),
            pltpu.SemaphoreType.DMA((4,)),
        ],
        compiler_params=params(),
        cost_estimate=pl.CostEstimate(
            flops=4 * rows * width * units, bytes_accessed=4 * width * units, transcendentals=0
        ),
    )(branches, current, gain, own, other)


def down_kernel(active_ref, own_ref, other_ref, out_ref, held, sems):
    part = own_ref.shape[0] // 2
    copies = []
    for i in range(4):
        source = (own_ref, other_ref)[i // 2].at[pl.ds((i % 2) * part, part)]
        copies.append(pltpu.make_async_copy(source, held.at[i], sems.at[i]))
        copies[-1].start()
    branch = jnp.zeros(out_ref.shape[1:], jnp.float32)
    for i in range(4):
        copies[i].wait()
        branch = branch + dot(active_ref[:, pl.ds(i * part, part)], held[i])
    out_ref[...] = jnp.broadcast_to(branch.astype(jnp.bfloat16)[None], out_ref.shape)


def down(active, own, other, copies):
    rows = active.shape[0]
    units, width = own.shape
    return pl.pallas_call(
        down_kernel,
        in_specs=[VMEM, ANYWHERE, ANYWHERE],
        out_specs=VMEM,
        out_shape=jax.ShapeDtypeStruct((copies, rows, width), jnp.bfloat16),
        scratch_shapes=[
            pltpu.VMEM((4, units // 2, width), jnp.bfloat16),
            pltpu.SemaphoreType.DMA((4,)),
        ],
        compiler_params=params(),
        cost_estimate=pl.CostEstimate(
            flops=4 * rows * width * units, bytes_accessed=4 * width * units, transcendentals=0
        ),
    )(active, own, other)


def per_device(stream, norm_gain, frozen_up_weight, factor_a, factor_b, down_projection_matrix):
    rows, width = stream.shape
    units = frozen_up_weight.shape[1]
    half = rows // 2
    first = lax.axis_index("tp") % 2 == 0
    gain = norm_gain[None]

    ranks_a = share(factor_a, "tp", None, 16)
    ranks_a = ranks_a.reshape(2, 4, 4, 2, width).transpose(1, 0, 2, 3, 4).reshape(-1, width)
    ranks = ranks_a.shape[0]

    ordered = stream.reshape(2, 8, rows // 16, width).transpose(1, 0, 2, 3).reshape(rows, width)
    scaled = (ordered * gain).astype(jnp.bfloat16)
    squares = jnp.sum(ordered * ordered, axis=1, keepdims=True)
    projected = lax.dot_general(
        scaled, ranks_a, (((1,), (1,)), ((), ())), preferred_element_type=jnp.float32
    )
    sent = pack(dot(scaled, frozen_up_weight), squares, projected).reshape(8, rows // 8, -1)
    end = sent.shape[2]
    own_b = jnp.pad(factor_b.reshape(8, units // 4), ((0, 0), (0, 512 - units // 4)))
    sent = jnp.concatenate([sent, jnp.broadcast_to(own_b[None], (8,) + own_b.shape)], axis=2)
    near = exchange(sent, "src", NEAR)
    near_sum = total(near[:, :, :end])
    values, squares = unpack(near_sum, units)
    projected = near_sum[:, units + 3 : units + 3 + ranks]
    sent = jnp.concatenate(
        [pack(values, squares, projected)] + [near[i, :, end:] for i in range(8)], axis=1
    )
    far = share(sent, "src", FAR, 4)
    far_sum = total(far[:, :, :end])
    ranks_b = far[:, :, end:].reshape(4, 8, 8, 512)[..., : units // 4]
    ranks_b = ranks_b.transpose(0, 2, 1, 3).reshape(ranks, units)
    values, squares = unpack(far_sum, units)
    projected = far_sum[:, units + 3 : units + 3 + ranks]
    high = lax.reduce_precision(projected, 8, 7)
    both = jnp.concatenate([high, projected - high], axis=0).astype(jnp.bfloat16)
    update = dot(both, ranks_b)
    update = update[: rows // 8] + update[rows // 8 :]
    active = activate(values + ADAPTER_SCALING * update, squares)

    down_own = down_projection_matrix
    down_other = lax.ppermute(down_own, "tp", SWAP)
    up_own = merge(frozen_up_weight, ranks_a, ranks_b)
    up_other = lax.ppermute(up_own, "tp", SWAP)

    sent = jnp.broadcast_to(
        active.reshape(2, 1, rows // 16, units), (2, 8, rows // 16, units)
    ).reshape(16, rows // 16, units)
    active = exchange(sent, ("src", "tp"), PAIRS).reshape(2, half, units)
    active = jnp.concatenate(
        [jnp.where(first, active[0], active[1]), jnp.where(first, active[1], active[0])], axis=1
    )
    current = jnp.where(first, stream[:half], stream[half:])
    branches = exchange(down(active, down_own, down_other, 8), "tp", CHIPS)

    for step in range(1, STEPS):
        current, sent = up(branches, current, gain, up_own, up_other)
        near = total(exchange(sent.reshape(8, half // 8, -1), "src", NEAR))
        far = total(share(pack(*unpack(near, 2 * units)), "src", FAR, 4))
        active = activate(*unpack(far, 2 * units))
        active = share(active, "src", NEAR, 8).reshape(half, 2 * units)
        branches = exchange(down(active, down_own, down_other, 8), "tp", CHIPS)
    current = current + total(branches)
    return share(current, "tp", CORES, 2).reshape(rows, width)


def solution(mesh):
    in_specs = (
        P(None, "src"),
        P("src"),
        P("src", "tp"),
        P("tp", "src"),
        P("src", "tp"),
        P("tp", "src"),
    )
    out_specs = P(None, "src")
    return jax.shard_map(
        per_device, mesh=mesh, in_specs=in_specs, out_specs=out_specs, check_vma=False
    )
```

```python
import jax
import jax.numpy as jnp
from jax import lax
from jax.experimental import pallas as pl
from jax.experimental.pallas import tpu as pltpu
from jax.sharding import PartitionSpec as P

D = 16384
STEPS = 3
LANES = 128

ADAPTER_SCALING = 2.0
EPSILON = 1e-05

NEAR = [[y * 16 + far * 4 + low for y in range(2) for low in range(4)] for far in range(4)]
FAR = [[y * 16 + far * 4 + low for far in range(4)] for y in range(2) for low in range(4)]
PAIRS = [
    [src * 16 + chip * 2 + core for core in range(2) for src in near]
    for near in NEAR
    for chip in range(8)
]
CORES = [[2 * chip, 2 * chip + 1] for chip in range(8)]
CHIPS = [[2 * chip + core for chip in range(8)] for core in range(2)]
SWAP = [(i, i ^ 1) for i in range(16)]


def exchange(blocks, axis, groups):
    return lax.all_to_all(blocks, axis, 0, 0, axis_index_groups=groups, tiled=True)


def share(block, axis, groups, size):
    return exchange(jnp.broadcast_to(block[None], (size,) + block.shape), axis, groups)


def total(blocks):
    return jnp.sum(blocks.astype(jnp.float32), axis=0)


def pack(values, squares, others=None):
    high = lax.reduce_precision(squares, 8, 7)
    rest = squares - high
    middle = lax.reduce_precision(rest, 8, 7)
    parts = [values, high, middle, rest - middle]
    used = 3
    if others is not None:
        parts.append(others)
        used += others.shape[1]
    parts.append(jnp.zeros((values.shape[0], LANES - used), jnp.float32))
    return jnp.concatenate(parts, axis=1).astype(jnp.bfloat16)


def unpack(both, width, ranks):
    squares = jnp.sum(both[:, width : width + 3], axis=1, keepdims=True)
    return both[:, :width], squares, both[:, width + 3 : width + 3 + ranks]


def activate(values, squares, projected, ranks_b):
    rows = values.shape[0]
    high = lax.reduce_precision(projected, 8, 7)
    both = jnp.concatenate([high, projected - high], axis=0).astype(jnp.bfloat16)
    update = dot(both, ranks_b)
    values = values + ADAPTER_SCALING * (update[:rows] + update[rows:])
    hidden = values * lax.rsqrt(squares / D + EPSILON)
    return jax.nn.silu(hidden).astype(jnp.bfloat16)


def dot(a, b):
    return jnp.dot(a, b, preferred_element_type=jnp.float32)


def params(mib=24):
    return pltpu.CompilerParams(vmem_limit_bytes=mib * 1024 * 1024)


VMEM = pl.BlockSpec(memory_space=pltpu.VMEM)
HBM = pl.BlockSpec(memory_space=pltpu.HBM)


def up_kernel(branch_ref, current_ref, gain_ref, a_ref, own_ref, other_ref, next_ref, sent_ref, held, sems):
    units = own_ref.shape[1]
    part = units // 2
    copies = []
    for i in range(2):
        source = other_ref.at[:, pl.ds(i * part, part)]
        copies.append(pltpu.make_async_copy(source, held.at[i], sems.at[i]))
        copies[-1].start()
    current = current_ref[...] + jnp.sum(branch_ref[...].astype(jnp.float32), axis=0)
    next_ref[...] = current
    scaled = (current * gain_ref[...]).astype(jnp.bfloat16)
    squares = jnp.sum(current * current, axis=1, keepdims=True)
    high = squares.astype(jnp.bfloat16).astype(jnp.float32)
    rest = squares - high
    middle = rest.astype(jnp.bfloat16).astype(jnp.float32)
    lane = lax.broadcasted_iota(jnp.int32, (current.shape[0], LANES), 1)
    tail = jnp.where(lane == 0, high, jnp.where(lane == 1, middle, rest - middle))
    tail = jnp.where(lane < 3, tail, dot(scaled, a_ref[...]))
    sent_ref[:, pl.ds(2 * units, LANES)] = tail.astype(jnp.bfloat16)
    sent_ref[:, pl.ds(0, units)] = dot(scaled, own_ref[...]).astype(jnp.bfloat16)
    for i in range(2):
        copies[i].wait()
        sent_ref[:, pl.ds(units + i * part, part)] = dot(scaled, held[i]).astype(jnp.bfloat16)


def up(branches, current, gain, columns_a, own, other):
    rows, width = current.shape
    units = own.shape[1]
    return pl.pallas_call(
        up_kernel,
        in_specs=[VMEM] * 5 + [HBM],
        out_specs=[VMEM, VMEM],
        out_shape=[
            jax.ShapeDtypeStruct(current.shape, jnp.float32),
            jax.ShapeDtypeStruct((rows, 2 * units + LANES), jnp.bfloat16),
        ],
        scratch_shapes=[
            pltpu.VMEM((2, width, units // 2), jnp.bfloat16),
            pltpu.SemaphoreType.DMA((2,)),
        ],
        compiler_params=params(),
        cost_estimate=pl.CostEstimate(
            flops=4 * rows * width * units, bytes_accessed=4 * width * units, transcendentals=0
        ),
    )(branches, current, gain, columns_a, own, other)


def down_kernel(active_ref, own_ref, other_ref, *refs):
    out_ref, held, sems = refs[-3:]
    part = own_ref.shape[0] // 2
    copies = []
    for i in range(4):
        source = (own_ref, other_ref)[i // 2].at[pl.ds((i % 2) * part, part)]
        copies.append(pltpu.make_async_copy(source, held.at[i], sems.at[i]))
        copies[-1].start()
    branch = jnp.zeros(out_ref.shape[1:], jnp.float32)
    for i in range(4):
        copies[i].wait()
        branch = branch + dot(active_ref[:, pl.ds(i * part, part)], held[i])
    out_ref[...] = jnp.broadcast_to(branch.astype(jnp.bfloat16)[None], out_ref.shape)


def down(active, own, other, copies, *after):
    rows = active.shape[0]
    units, width = own.shape
    return pl.pallas_call(
        down_kernel,
        in_specs=[VMEM, HBM, HBM] + [pl.BlockSpec(memory_space=pl.ANY)] * len(after),
        out_specs=VMEM,
        out_shape=jax.ShapeDtypeStruct((copies, rows, width), jnp.bfloat16),
        scratch_shapes=[
            pltpu.VMEM((4, units // 2, width), jnp.bfloat16),
            pltpu.SemaphoreType.DMA((4,)),
        ],
        compiler_params=params(52),
        cost_estimate=pl.CostEstimate(
            flops=4 * rows * width * units, bytes_accessed=4 * width * units, transcendentals=0
        ),
    )(active, own, other, *after)


def per_device(stream, norm_gain, frozen_up_weight, factor_a, factor_b, down_projection_matrix):
    rows, width = stream.shape
    units = frozen_up_weight.shape[1]
    half = rows // 2
    first = lax.axis_index("tp") % 2 == 0
    gain = norm_gain[None]

    up_own, down_own = frozen_up_weight, down_projection_matrix
    up_other = lax.ppermute(up_own, "tp", SWAP)
    down_other = lax.ppermute(down_own, "tp", SWAP)

    ranks_a = share(factor_a, "tp", None, 16).reshape(-1, width)
    ranks = ranks_a.shape[0]
    columns_a = jnp.pad(ranks_a.T, ((0, 0), (3, LANES - 3 - ranks)))

    scaled = (stream * gain).astype(jnp.bfloat16)
    squares = jnp.sum(stream * stream, axis=1, keepdims=True)
    projected = dot(scaled, columns_a)[:, 3 : 3 + ranks]
    sent = pack(dot(scaled, up_own), squares, projected).reshape(8, rows // 8, -1)
    end = sent.shape[2]
    quarter = units // 4
    own_b = factor_b.reshape(8, quarter)
    own_b = jnp.pad(own_b, ((0, 0), (0, -(end + quarter) % LANES)))
    sent = jnp.concatenate([sent, jnp.broadcast_to(own_b[None], (8,) + own_b.shape)], axis=2)
    near = exchange(sent, "src", NEAR)
    sent = pack(*unpack(total(near[:, :, :end]), units, ranks))
    sent = jnp.concatenate(
        [sent] + [near[i, :, end : end + quarter] for i in range(8)], axis=1
    )
    far = share(sent, "src", FAR, 4)
    own_b = far[:, :, end:].reshape(4, 8, 2, 4, quarter).transpose(2, 0, 3, 1, 4)
    own_b = own_b.reshape(ranks, units)
    active = activate(*unpack(total(far[:, :, :end]), units, ranks), own_b)
    other_b = lax.ppermute(own_b, "tp", SWAP)
    ranks_b = jnp.concatenate([own_b, other_b], axis=1)

    sent = jnp.broadcast_to(
        active.reshape(2, 1, rows // 16, units), (2, 8, rows // 16, units)
    ).reshape(16, rows // 16, units)
    active = exchange(sent, ("src", "tp"), PAIRS).reshape(2, half, units)
    active = jnp.concatenate(
        [jnp.where(first, active[0], active[1]), jnp.where(first, active[1], active[0])], axis=1
    )
    by_core = stream.reshape(8, 2, rows // 16, width)
    current = jnp.where(first, by_core[:, 0], by_core[:, 1]).reshape(half, width)
    branches = down(active, down_own, down_other, 8, up_other, ranks_b, current)
    branches = exchange(branches, "tp", CHIPS)

    for step in range(1, STEPS):
        current, sent = up(branches, current, gain, columns_a, up_own, up_other)
        near = total(exchange(sent.reshape(8, half // 8, -1), "src", NEAR))
        far = total(share(pack(*unpack(near, 2 * units, ranks)), "src", FAR, 4))
        active = activate(*unpack(far, 2 * units, ranks), ranks_b)
        active = share(active, "src", NEAR, 8).reshape(half, 2 * units)
        branches = exchange(down(active, down_own, down_other, 8), "tp", CHIPS)
    current = current + total(branches)
    by_core = share(current, "tp", CORES, 2).reshape(2, 8, rows // 16, width)
    return by_core.transpose(1, 0, 2, 3).reshape(rows, width)


def solution(mesh):
    in_specs = (
        P(None, "src"),
        P("src"),
        P("src", "tp"),
        P("tp", "src"),
        P("src", "tp"),
        P("tp", "src"),
    )
    out_specs = P(None, "src")
    return jax.shard_map(
        per_device, mesh=mesh, in_specs=in_specs, out_specs=out_specs, check_vma=False
    )
```

```python
import jax
import jax.numpy as jnp
from jax import lax
from jax.experimental import pallas as pl
from jax.experimental.pallas import tpu as pltpu
from jax.sharding import PartitionSpec as P

D = 16384
STEPS = 3
LANES = 128

ADAPTER_SCALING = 2.0
EPSILON = 1e-05

NEAR = [[y * 16 + far * 4 + low for y in range(2) for low in range(4)] for far in range(4)]
FAR = [[y * 16 + far * 4 + low for far in range(4)] for y in range(2) for low in range(4)]
PAIRS = [
    [src * 16 + chip * 2 + core for core in range(2) for src in near]
    for near in NEAR
    for chip in range(8)
]
CHIPS = [[2 * chip + core for chip in range(8)] for core in range(2)]
SWAP = [(i, i ^ 1) for i in range(16)]


def exchange(blocks, axis, groups):
    return lax.all_to_all(blocks, axis, 0, 0, axis_index_groups=groups, tiled=True)


def share(block, axis, groups, size):
    return exchange(jnp.broadcast_to(block[None], (size,) + block.shape), axis, groups)


def total(blocks):
    return jnp.sum(blocks.astype(jnp.float32), axis=0)


def pack(values, squares, others=None):
    high = lax.reduce_precision(squares, 8, 7)
    rest = squares - high
    middle = lax.reduce_precision(rest, 8, 7)
    parts = [values, high, middle, rest - middle]
    used = 3
    if others is not None:
        parts.append(others)
        used += others.shape[1]
    parts.append(jnp.zeros((values.shape[0], LANES - used), jnp.float32))
    return jnp.concatenate(parts, axis=1).astype(jnp.bfloat16)


def unpack(both, width, ranks):
    squares = jnp.sum(both[:, width : width + 3], axis=1, keepdims=True)
    return both[:, :width], squares, both[:, width + 3 : width + 3 + ranks]


def activate(values, squares, projected, ranks_b):
    rows = values.shape[0]
    high = lax.reduce_precision(projected, 8, 7)
    both = jnp.concatenate([high, projected - high], axis=0).astype(jnp.bfloat16)
    update = dot(both, ranks_b)
    values = values + ADAPTER_SCALING * (update[:rows] + update[rows:])
    hidden = values * lax.rsqrt(squares / D + EPSILON)
    return jax.nn.silu(hidden).astype(jnp.bfloat16)


def dot(a, b):
    return jnp.dot(a, b, preferred_element_type=jnp.float32)


def params(mib=24):
    return pltpu.CompilerParams(vmem_limit_bytes=mib * 1024 * 1024)


VMEM = pl.BlockSpec(memory_space=pltpu.VMEM)
HBM = pl.BlockSpec(memory_space=pltpu.HBM)


def up_kernel(branch_ref, current_ref, gain_ref, a_ref, own_ref, other_ref, next_ref, sent_ref, held, sems):
    width, units = own_ref.shape
    part = width // 2
    copies = []
    for i in range(2):
        source = other_ref.at[pl.ds(i * part, part)]
        copies.append(pltpu.make_async_copy(source, held.at[i], sems.at[i]))
        copies[-1].start()
    current = current_ref[...] + jnp.sum(branch_ref[...].astype(jnp.float32), axis=0)
    next_ref[...] = current
    scaled = (current * gain_ref[...]).astype(jnp.bfloat16)
    squares = jnp.sum(current * current, axis=1, keepdims=True)
    high = squares.astype(jnp.bfloat16).astype(jnp.float32)
    rest = squares - high
    middle = rest.astype(jnp.bfloat16).astype(jnp.float32)
    lane = lax.broadcasted_iota(jnp.int32, (current.shape[0], LANES), 1)
    tail = jnp.where(lane == 0, high, jnp.where(lane == 1, middle, rest - middle))
    tail = jnp.where(lane < 3, tail, dot(scaled, a_ref[...]))
    sent_ref[:, pl.ds(2 * units, LANES)] = tail.astype(jnp.bfloat16)
    sent_ref[:, pl.ds(0, units)] = dot(scaled, own_ref[...]).astype(jnp.bfloat16)
    values = jnp.zeros((current.shape[0], units), jnp.float32)
    for i in range(2):
        copies[i].wait()
        values = values + dot(scaled[:, i * part : (i + 1) * part], held[i])
    sent_ref[:, pl.ds(units, units)] = values.astype(jnp.bfloat16)


def up(branches, current, gain, columns_a, own, other):
    rows, width = current.shape
    units = own.shape[1]
    return pl.pallas_call(
        up_kernel,
        in_specs=[VMEM] * 5 + [HBM],
        out_specs=[VMEM, VMEM],
        out_shape=[
            jax.ShapeDtypeStruct(current.shape, jnp.float32),
            jax.ShapeDtypeStruct((rows, 2 * units + LANES), jnp.bfloat16),
        ],
        scratch_shapes=[
            pltpu.VMEM((2, width // 2, units), jnp.bfloat16),
            pltpu.SemaphoreType.DMA((2,)),
        ],
        compiler_params=params(),
        cost_estimate=pl.CostEstimate(
            flops=4 * rows * width * units, bytes_accessed=4 * width * units, transcendentals=0
        ),
    )(branches, current, gain, columns_a, own, other)


def down_kernel(active_ref, own_ref, other_ref, *refs):
    out_ref, held, sems = refs[-3:]
    part = own_ref.shape[0] // 2
    copies = []
    for i in range(4):
        source = (own_ref, other_ref)[i // 2].at[pl.ds((i % 2) * part, part)]
        copies.append(pltpu.make_async_copy(source, held.at[i], sems.at[i]))
        copies[-1].start()
    branch = jnp.zeros(out_ref.shape[1:], jnp.float32)
    for i in range(4):
        copies[i].wait()
        branch = branch + dot(active_ref[:, pl.ds(i * part, part)], held[i])
    out_ref[...] = jnp.broadcast_to(branch.astype(jnp.bfloat16)[None], out_ref.shape)


def down(active, own, other, copies, *after):
    rows = active.shape[0]
    units, width = own.shape
    return pl.pallas_call(
        down_kernel,
        in_specs=[VMEM, HBM, HBM] + [pl.BlockSpec(memory_space=pl.ANY)] * len(after),
        out_specs=VMEM,
        out_shape=jax.ShapeDtypeStruct((copies, rows, width), jnp.bfloat16),
        scratch_shapes=[
            pltpu.VMEM((4, units // 2, width), jnp.bfloat16),
            pltpu.SemaphoreType.DMA((4,)),
        ],
        compiler_params=params(52),
        cost_estimate=pl.CostEstimate(
            flops=4 * rows * width * units, bytes_accessed=4 * width * units, transcendentals=0
        ),
    )(active, own, other, *after)


def per_device(stream, norm_gain, frozen_up_weight, factor_a, factor_b, down_projection_matrix):
    rows, width = stream.shape
    units = frozen_up_weight.shape[1]
    half = rows // 2
    first = lax.axis_index("tp") % 2 == 0
    gain = norm_gain[None]

    up_own, down_own = frozen_up_weight, down_projection_matrix
    up_other = lax.ppermute(up_own, "tp", SWAP)
    down_other = lax.ppermute(down_own, "tp", SWAP)

    ranks_a = share(factor_a, "tp", None, 16).reshape(-1, width)
    ranks = ranks_a.shape[0]
    columns_a = jnp.pad(ranks_a.T, ((0, 0), (3, LANES - 3 - ranks)))

    scaled = (stream * gain).astype(jnp.bfloat16)
    squares = jnp.sum(stream * stream, axis=1, keepdims=True)
    projected = dot(scaled, columns_a)[:, 3 : 3 + ranks]
    sent = pack(dot(scaled, up_own), squares, projected).reshape(8, rows // 8, -1)
    end = sent.shape[2]
    quarter = units // 4
    own_b = factor_b.reshape(8, quarter)
    own_b = jnp.pad(own_b, ((0, 0), (0, -(end + quarter) % LANES)))
    sent = jnp.concatenate([sent, jnp.broadcast_to(own_b[None], (8,) + own_b.shape)], axis=2)
    near = exchange(sent, "src", NEAR)
    sent = pack(*unpack(total(near[:, :, :end]), units, ranks))
    sent = jnp.concatenate(
        [sent] + [near[i, :, end : end + quarter] for i in range(8)], axis=1
    )
    far = share(sent, "src", FAR, 4)
    own_b = far[:, :, end:].reshape(4, 8, 2, 4, quarter).transpose(2, 0, 3, 1, 4)
    own_b = own_b.reshape(ranks, units)
    active = activate(*unpack(total(far[:, :, :end]), units, ranks), own_b)
    other_b = lax.ppermute(own_b, "tp", SWAP)
    ranks_b = jnp.concatenate([own_b, other_b], axis=1)

    sent = jnp.broadcast_to(
        active.reshape(2, 1, rows // 16, units), (2, 8, rows // 16, units)
    ).reshape(16, rows // 16, units)
    active = exchange(sent, ("src", "tp"), PAIRS).reshape(2, half, units)
    active = jnp.concatenate(
        [jnp.where(first, active[0], active[1]), jnp.where(first, active[1], active[0])], axis=1
    )
    by_core = stream.reshape(8, 2, rows // 16, width)
    current = jnp.where(first, by_core[:, 0], by_core[:, 1]).reshape(half, width)
    branches = down(active, down_own, down_other, 8, up_other, ranks_b, current)
    branches = exchange(branches, "tp", CHIPS)

    for step in range(1, STEPS):
        current, sent = up(branches, current, gain, columns_a, up_own, up_other)
        near = total(exchange(sent.reshape(8, half // 8, -1), "src", NEAR))
        far = total(share(pack(*unpack(near, 2 * units, ranks)), "src", FAR, 4))
        active = activate(*unpack(far, 2 * units, ranks), ranks_b)
        active = share(active, "src", NEAR, 8).reshape(half, 2 * units)
        branches = exchange(down(active, down_own, down_other, 8), "tp", CHIPS)
    current = current + total(branches)
    own = current.reshape(8, rows // 16, width)
    other = lax.ppermute(current, "tp", SWAP).reshape(8, rows // 16, width)
    by_core = [jnp.where(first, own, other), jnp.where(first, other, own)]
    return jnp.stack(by_core, axis=1).reshape(rows, width)


def solution(mesh):
    in_specs = (
        P(None, "src"),
        P("src"),
        P("src", "tp"),
        P("tp", "src"),
        P("src", "tp"),
        P("tp", "src"),
    )
    out_specs = P(None, "src")
    return jax.shard_map(
        per_device, mesh=mesh, in_specs=in_specs, out_specs=out_specs, check_vma=False
    )
```
